32 devices in a mesh: section: 8 (over z, x), dp: 4 (over y, core).
Axes of the slice: x: 2, y: 2, z: 4, core: 2. Of those that a mesh axis runs over, the one named last changes fastest.
Arguments:
- queries: bfloat16 [8, 1536, 1024], P('section', 'dp'), may hold values from -600 to 600
- images: bfloat16 [4, 128, 8192], P('dp', 'section'), may hold values from -6 to 6
- w_key: bfloat16 [8, 8192, 128], P('section', 'dp'), may hold values from -0.0625 to 0.0625
- w_value: bfloat16 [8, 8192, 128], P('section', 'dp'), may hold values from -0.0625 to 0.0625
- key_gain: float32 [2, 128], replicated, may hold values from 0.1 to 1.9
- d_out: bfloat16 [8, 1536, 1024], P('section', 'dp'), may hold values from -6 to 6
- img_len: int32 [4], P('dp'), may hold values from 32 to 128, as said below
- text_start: int32 [4], P('dp'), may hold values from 0 to 191
Outputs:
- attended: bfloat16 [8, 1536, 1024], P('section', 'dp')
- d_images: float32 [4, 128, 8192], P('dp', 'section')
The draws below stay inside these ranges and needn't reach their ends.
Inputs may be any that keep to these rules, and one draw needn't show every extreme that they name: `img_len`: each sample uses a whole number of tiles of 32 tokens, 1 to 4 tiles; some sample uses all 4.
All inputs are finite; a program needn't handle non-finite values.
Results may differ from the reference program's by a relative error of at most 0.025.
Values may be sent and summed in bfloat16 or wider, within the bound.
A program may use at most 64 MiB of HBM per device.

```python
import math
import jax
import jax.numpy as jnp
from jax import lax

D = 8192
HEAD = 128
KVH = 4
IMG_TOK = 128
TXT_DEV = 384
LAYERS = 2
LAYER_HEADS = 8
GROUPS = 4
TEXT = 1536
QW = 1024


def draw_queries(key, part):
    base = jnp.clip(jax.random.normal(key, (LAYER_HEADS, TEXT, QW), jnp.float32), -5.0, 5.0)
    return base.astype(jnp.bfloat16)


def draw_d_out(key, part):
    base = jnp.clip(jax.random.normal(jax.random.fold_in(key, 11), (LAYER_HEADS, TEXT, QW), jnp.float32), -6.0, 6.0)
    return base.astype(jnp.bfloat16)


def draw_img_len(key, part):
    tiles = jax.random.randint(key, (GROUPS,), 1, 5)
    chosen = jax.random.randint(jax.random.fold_in(key, 3), (), 0, GROUPS)
    tiles = jnp.where(jnp.arange(GROUPS) == chosen, 4, tiles)
    return (tiles * (IMG_TOK // 4)).astype(jnp.int32)


def plant(drawn, key, least, high):
    extent = drawn.shape
    index_at = [jax.random.randint(jax.random.fold_in(key, axis), (), 0, extent[axis]) for axis in range(len(extent))]
    drawn = drawn.at[tuple(index_at)].set(least)
    longest = extent.index(max(extent))
    index_at[longest] = (index_at[longest] + 1) % extent[longest]
    return drawn.at[tuple(index_at)].set(high)


def shard_levels(stream_key, shape, shards, least, largest):
    def one(axis_at, shards_of):
        draws = jax.random.uniform(jax.random.fold_in(jax.random.fold_in(stream_key, 6), axis_at), (shards_of,), jnp.float32, least / len(shards), largest / len(shards))
        return jnp.repeat(jnp.exp(draws), shape[axis_at] // shards_of).reshape((-1,) + (1,) * (len(shape) - axis_at - 1))

    level = one(*shards[0])
    for cut in shards[1:]:
        level = level * one(*cut)
    return level


def normal_values(rng, shape, scale, reach, pieces=(), dtype=jnp.bfloat16):
    values = scale * jax.random.normal(rng, shape, jnp.float32)
    if pieces:
        values = values * shard_levels(rng, shape, pieces, -0.22, 0.18)
    return jnp.clip(values, -reach, reach).astype(dtype)


def setup_inputs(seed: int = 0) -> dict:
    key_list = jax.random.split(jax.random.key(seed), 9)
    return {
        "queries": draw_queries(jax.random.fold_in(key_list[8], 71), 0),
        "images": normal_values(key_list[1], (GROUPS, IMG_TOK, D), 1.0, 6.0, ((0, 4), (1, 8))),
        "w_key": normal_values(key_list[2], (LAYER_HEADS, D, HEAD), D ** -0.5, 0.0625, ((0, 8), (1, 4))),
        "w_value": normal_values(key_list[3], (LAYER_HEADS, D, HEAD), D ** -0.5, 0.0625, ((0, 8), (1, 4))),
        "key_gain": jnp.clip(1.0 + 0.18 * jax.random.normal(key_list[4], (LAYERS, HEAD), jnp.float32), 0.1, 1.9),
        "d_out": draw_d_out(jax.random.fold_in(key_list[8], 71), 0),
        "img_len": draw_img_len(jax.random.fold_in(key_list[8], 71), 0),
        "text_start": plant(jax.random.randint(key_list[7], (GROUPS,), 0, TXT_DEV // 2), jax.random.fold_in(key_list[7], 1), 0, (TXT_DEV // 2) - 1).astype(jnp.int32),
    }


def attend(key_raw, value_raw, key_gain, queries, length, start):
    inverse = lax.rsqrt(lax.optimization_barrier(jnp.mean(key_raw * key_raw, axis=-1, keepdims=True)) + 1e-05)
    keys = (key_raw * inverse * key_gain).astype(jnp.bfloat16)
    values = value_raw.astype(jnp.bfloat16)
    head_size = key_gain.shape[-1]
    heads = queries.reshape(queries.shape[0], -1, head_size).astype(jnp.float32)
    scores = jnp.einsum('thd,jd->htj', heads, keys.astype(jnp.float32)) / math.sqrt(head_size)
    usable = jnp.arange(keys.shape[0]) < length
    scores = jnp.where(usable, scores, -1e+30)
    scores = scores - lax.optimization_barrier(jnp.max(scores, axis=-1, keepdims=True))
    expo = jnp.exp(scores)
    probs = (expo / lax.optimization_barrier(jnp.sum(expo, axis=-1, keepdims=True))).astype(jnp.bfloat16)
    mixed = jnp.einsum('htj,jd->thd', probs.astype(jnp.float32), values.astype(jnp.float32))
    mixed = mixed.reshape(queries.shape[0], -1)
    shown = jnp.arange(queries.shape[0]) >= start
    return jnp.where(shown[:, None], mixed, 0.0)

def one_sample(image_rows, key_weight, value_weight, gain, query_rows, cotangent, length, start):
    key_raw = jnp.dot(image_rows, key_weight, preferred_element_type=jnp.float32)
    value_raw = jnp.dot(image_rows, value_weight, preferred_element_type=jnp.float32)
    mixed, pull_back = jax.vjp(lambda kr, vr: attend(kr, vr, gain, query_rows, length, start), key_raw, value_raw)
    d_key, d_value = pull_back(cotangent.astype(jnp.float32))
    term = jnp.dot(d_key.astype(jnp.bfloat16), key_weight.T, preferred_element_type=jnp.float32)
    term = term + jnp.dot(d_value.astype(jnp.bfloat16), value_weight.T, preferred_element_type=jnp.float32)
    rounded = lax.optimization_barrier(term.astype(jnp.bfloat16))
    return (mixed.astype(jnp.bfloat16), rounded.astype(jnp.float32))

def reference(queries, images, w_key, w_value, key_gain, d_out, img_len, text_start):
    query_blocks = queries.reshape(LAYER_HEADS, GROUPS, TXT_DEV, QW)
    grad_blocks = d_out.reshape(LAYER_HEADS, GROUPS, TXT_DEV, QW)
    gains = jnp.repeat(key_gain, KVH, axis=0)

    def per_head(total, items):
        query_section, grad_section, key_weight, value_weight, gain = items
        mixed, terms = jax.vmap(lambda rows, qrows, grows, length, start: one_sample(rows, key_weight, value_weight, gain, qrows, grows, length, start))(images, query_section, grad_section, img_len, text_start)
        return (total + terms, mixed)
    start_total = jnp.zeros((GROUPS, IMG_TOK, D), jnp.float32)
    total, outputs = lax.scan(per_head, start_total, (query_blocks, grad_blocks, w_key, w_value, gains))
    return (outputs.reshape(LAYER_HEADS, TEXT, QW), total)
```

```python
import functools
import math

import jax
import jax.numpy as jnp
from jax import lax
from jax.experimental import pallas as pl
from jax.experimental.pallas import tpu as pltpu
from jax.sharding import PartitionSpec as P

MESH = pl.DeviceIdType.MESH
PARTS = 2
BF = jnp.bfloat16
F32 = jnp.float32


def attend(key_raw, value_raw, key_gain, queries, length, start):
    inverse = lax.rsqrt(jnp.mean(key_raw * key_raw, axis=-1, keepdims=True) + 1e-05)
    keys = (key_raw * inverse * key_gain).astype(jnp.bfloat16)
    values = value_raw.astype(jnp.bfloat16)
    head_size = key_gain.shape[-1]
    heads = queries.reshape(queries.shape[0], -1, head_size).astype(jnp.float32)
    scores = jnp.einsum("thd,jd->htj", heads, keys.astype(jnp.float32)) / math.sqrt(head_size)
    usable = jnp.arange(keys.shape[0]) < length
    scores = jnp.where(usable, scores, -1e30)
    scores = scores - jnp.max(scores, axis=-1, keepdims=True)
    expo = jnp.exp(scores)
    probs = (expo / jnp.sum(expo, axis=-1, keepdims=True)).astype(jnp.bfloat16)
    mixed = jnp.einsum("htj,jd->thd", probs.astype(jnp.float32), values.astype(jnp.float32))
    mixed = mixed.reshape(queries.shape[0], -1)
    shown = jnp.arange(queries.shape[0]) >= start
    return jnp.where(shown[:, None], mixed, 0.0)


def plain(layer_heads, queries, images, w_key, w_value, key_gain, d_out, img_len, text_start):
    image_full = lax.all_gather(images[0], "section", axis=0, tiled=True)
    layer = lax.axis_index("section") // layer_heads
    gain = lax.dynamic_index_in_dim(key_gain, layer, 0, keepdims=False)
    key_weight = lax.all_gather(w_key[0], "dp", axis=0, tiled=True)
    value_weight = lax.all_gather(w_value[0], "dp", axis=0, tiled=True)
    key_raw = jnp.dot(image_full, key_weight, preferred_element_type=jnp.float32)
    value_raw = jnp.dot(image_full, value_weight, preferred_element_type=jnp.float32)
    mixed, pull_back = jax.vjp(
        lambda kr, vr: attend(kr, vr, gain, queries[0], img_len[0], text_start[0]), key_raw, value_raw
    )
    d_key, d_value = pull_back(d_out[0].astype(jnp.float32))
    term = jnp.dot(d_key.astype(BF), key_weight.T, preferred_element_type=jnp.float32)
    term = term + jnp.dot(d_value.astype(BF), value_weight.T, preferred_element_type=jnp.float32)
    own = lax.psum_scatter(term.astype(BF), "section", scatter_dimension=0, tiled=True)
    return mixed.astype(BF)[None], own.astype(jnp.float32)[None]


def nt(a, b):
    return lax.dot_general(a, b, (((1,), (1,)), ((), ())), preferred_element_type=F32)


def kernel(
    n, m, layer_heads,
    len_ref, start_ref, gain_ref, q_hbm, img_hbm, wk_hbm, wv_hbm, do_hbm,
    att_ref, grad_ref,
    img, wk, wv, q, do, probs, term, stage, recv, kraw, vraw, dk, dv,
    local_sem, ag_send, ag_recv, w_send, w_recv, rs_send, rs_recv,
):
    half = n // 2
    s = lax.axis_index("section")
    g = lax.axis_index("dp")
    x = lax.rem(s, 2)
    pos = (1 - x) * lax.div(s, 2) + x * (n - 1 - lax.div(s, 2))

    def sec(offset):
        at = lax.rem(pos + offset + n, n)
        hi = lax.div(at, half)
        return (1 - hi) * 2 * at + hi * (2 * (n - 1 - at) + 1)

    def dp_flip(bit):
        return g + bit - 2 * bit * lax.rem(lax.div(g, bit), 2)

    def dp_xor(mask):
        at = g
        for k in range(m.bit_length() - 1):
            if mask & (1 << k):
                at = at + (1 << k) - 2 * (1 << k) * lax.rem(lax.div(g, 1 << k), 2)
        return at

    bits = [1 << k for k in reversed(range(m.bit_length() - 1))]
    right, left = sec(1), sec(-1)
    barrier = pltpu.get_barrier_semaphore()
    for neighbour in (left, right):
        pl.semaphore_signal(barrier, inc=1, device_id={"section": neighbour}, device_id_type=MESH)
    for bit in bits:
        pl.semaphore_signal(barrier, inc=1, device_id={"dp": dp_flip(bit)}, device_id_type=MESH)

    locals_ = [
        pltpu.make_async_copy(img_hbm.at[0], img.at[s], local_sem.at[0]),
        pltpu.make_async_copy(wk_hbm.at[0], wk.at[g], local_sem.at[1]),
        pltpu.make_async_copy(wv_hbm.at[0], wv.at[g], local_sem.at[2]),
        pltpu.make_async_copy(q_hbm.at[0], q, local_sem.at[3]),
        pltpu.make_async_copy(do_hbm.at[0], do, local_sem.at[4]),
    ]
    for copy in locals_:
        copy.start()
    pl.semaphore_wait(barrier, 2 + len(bits))

    cols = img.shape[2]
    part = cols // PARTS
    to = (right, left)

    def ag_copy(way, step, c):
        block = sec(-step if way == 0 else step)
        here = pl.ds(c * part, part)
        source = img_hbm.at[0, :, here] if step == 0 else img.at[block, :, here]
        return pltpu.make_async_remote_copy(
            src_ref=source,
            dst_ref=img.at[block, :, here],
            send_sem=ag_send.at[way, step, c],
            recv_sem=ag_recv.at[way, step, c],
            device_id={"section": to[way]},
            device_id_type=MESH,
        )

    def ag_arrival(way, step, c):
        block = sec(-step - 1 if way == 0 else step + 1)
        here = pl.ds(c * part, part)
        return pltpu.make_async_remote_copy(
            src_ref=img.at[block, :, here],
            dst_ref=img.at[block, :, here],
            send_sem=ag_send.at[way, step, c],
            recv_sem=ag_recv.at[way, step, c],
            device_id={"section": to[way]},
            device_id_type=MESH,
        )

    def ag_parts(way, step):
        if step < half - 1:
            return range(PARTS)
        cut = PARTS // 2
        return range(cut) if way == 0 else range(cut, PARTS)

    w_list = []
    held = [0]
    for stage_at, bit in enumerate(bits):
        for mask in list(held):
            for which in range(2):
                w_list.append((stage_at, bit, mask, which))
            held.append(mask | bit)
    w_index = {(bit, mask, which): k for k, (_, bit, mask, which) in enumerate(w_list)}

    def w_copy(bit, mask, which):
        k = w_index[(bit, mask, which)]
        block = dp_xor(mask)
        full, mine = ((wk, wk_hbm), (wv, wv_hbm))[which]
        return pltpu.make_async_remote_copy(
            src_ref=mine.at[0] if mask == 0 else full.at[block],
            dst_ref=full.at[block],
            send_sem=w_send.at[k],
            recv_sem=w_recv.at[k],
            device_id={"dp": dp_flip(bit)},
            device_id_type=MESH,
        )

    def w_arrival(bit, mask, which):
        k = w_index[(bit, mask, which)]
        block = dp_xor(mask | bit)
        full = (wk, wv)[which]
        return pltpu.make_async_remote_copy(
            src_ref=full.at[block],
            dst_ref=full.at[block],
            send_sem=w_send.at[k],
            recv_sem=w_recv.at[k],
            device_id={"dp": dp_flip(bit)},
            device_id_type=MESH,
        )

    for bit in bits:
        if bit == bits[0]:
            for which in range(2):
                w_copy(bit, 0, which).start()
    for c in range(PARTS):
        for way in range(2):
            if c in ag_parts(way, 0):
                ag_copy(way, 0, c).start()
    for bit in bits[1:]:
        for which in range(2):
            w_copy(bit, 0, which).start()
    for step in range(1, half):
        for c in range(PARTS):
            for way in range(2):
                if c in ag_parts(way, step - 1):
                    ag_arrival(way, step - 1, c).wait_recv()
                    if c in ag_parts(way, step):
                        ag_copy(way, step, c).start()
    for way in range(2):
        for c in ag_parts(way, half - 1):
            ag_arrival(way, half - 1, c).wait_recv()
    for copy in locals_:
        copy.wait()

    depth = wk.shape[1]
    tokens = n * img.shape[1]

    def project(mask, which):
        block = dp_xor(mask)
        columns = pl.ds(pl.multiple_of(block * depth, depth), depth)
        rows = img[:, :, columns].reshape(tokens, depth)
        full, raw = ((wk, kraw), (wv, vraw))[which]
        value = jnp.dot(rows, full[block], preferred_element_type=F32)
        if mask == 0:
            raw[...] = value
        else:
            raw[...] += value

    for which in range(2):
        project(0, which)
    pending = []
    for bit in reversed(bits):
        lower = [b for b in bits if b < bit]
        for which in range(2):
            w_arrival(bit, 0, which).wait_recv()
            for low in lower:
                w_copy(low, bit, which).start()
            project(bit, which)
    for stage_at, bit, mask, which in w_list:
        if mask:
            pending.append((bit, mask, which))
    for bit, mask, which in pending:
        w_arrival(bit, mask, which).wait_recv()
        for low in [b for b in bits if b < bit]:
            w_copy(low, mask | bit, which).start()
        project(mask | bit, which)

    size = kraw.shape[1]
    text = q.shape[0]
    heads = q.shape[1] // size
    layer = lax.div(s, layer_heads)
    gain = gain_ref[pl.ds(layer, 1), :]
    key_raw = kraw[...]
    inverse = lax.rsqrt(jnp.mean(key_raw * key_raw, axis=-1, keepdims=True) + 1e-05)
    keys = (key_raw * inverse * gain).astype(BF)
    values = vraw[...].astype(BF)
    usable = lax.broadcasted_iota(jnp.int32, (tokens, text), 0) < len_ref[0]
    shown = lax.broadcasted_iota(jnp.int32, (1, text), 1) >= start_ref[0]
    scale = 1.0 / math.sqrt(size)
    scale2 = scale * math.log2(math.e)
    dk[...] = jnp.zeros_like(dk)
    dv[...] = jnp.zeros_like(dv)

    def one_head(h):
        at = pl.ds(pl.multiple_of(h * size, size), size)
        qh = q[:, at]
        doh = do[:, at]
        scores = jnp.where(usable, nt(keys, qh) * scale2, -1e30)
        expo = jnp.exp2(scores - jnp.max(scores, axis=0, keepdims=True))
        factor = jnp.where(shown, 1.0 / jnp.sum(expo, axis=0, keepdims=True), 0.0)
        p = expo * factor
        half_p = p.astype(BF)
        probs[h] = half_p
        d_p = nt(values, doh).astype(BF).astype(F32)
        d_s = (p * (d_p - jnp.sum(p * d_p, axis=0, keepdims=True))).astype(BF)
        return (
            jnp.dot(d_s, qh, preferred_element_type=F32),
            jnp.dot(half_p, doh, preferred_element_type=F32),
        )

    def pair(i, carry):
        k0, v0 = one_head(2 * i)
        k1, v1 = one_head(2 * i + 1)
        dk[...] += k0 + k1
        dv[...] += v0 + v1
        return carry

    lax.fori_loop(0, heads // 2, pair, 0)
    d_keys = (dk[...] * scale).astype(BF).astype(F32) * gain
    d_key = inverse * (d_keys - key_raw * (inverse * inverse) * jnp.mean(d_keys * key_raw, axis=-1, keepdims=True))
    d_key = d_key.astype(BF)
    d_value = dv[...].astype(BF)

    rows = img.shape[1]
    first = (list(range(m // 2)), list(range(m // 2, m)))
    later = (first[1] + first[0], first[0] + first[1])

    def rs_copy(way, step, c, source):
        here = pl.ds(c * depth, depth)
        return pltpu.make_async_remote_copy(
            src_ref=source.at[:, here],
            dst_ref=recv.at[way, step, :, here],
            send_sem=rs_send.at[way, step, c],
            recv_sem=rs_recv.at[way, step, c],
            device_id={"section": to[way]},
            device_id_type=MESH,
        )

    def target(way, step):
        return sec(half - step if way == 0 else step - half)

    order = [c for both in zip(*first) for c in both]
    for c in order:
        here = pl.ds(c * depth, depth)
        value = nt(d_key, wk[c]) + nt(d_value, wv[c])
        term[:, :, here] = value.astype(BF).reshape(n, rows, depth)
        for way in range(2):
            step = 0 if c in first[way] else 1
            if step < half:
                rs_copy(way, step, c, term.at[target(way, step)]).start()

    def mix(h):
        at = pl.ds(h * size, size)
        att_ref[0, :, at] = lax.dot_general(
            probs[h], values, (((0,), (0,)), ((), ())), preferred_element_type=F32
        ).astype(BF)

    to_mix = list(range(heads))
    for step in range(1, half):
        for k in range(m):
            if to_mix:
                mix(to_mix.pop(0))
            for way in range(2):
                c = later[way][k]
                if step == 1 and c not in first[way]:
                    continue
                here = pl.ds(c * depth, depth)
                rs_copy(way, step - 1, c, stage.at[way, step]).wait_recv()
                total = term[target(way, step), :, here].astype(F32) + recv[way, step - 1, :, here].astype(F32)
                stage[way, step, :, here] = total.astype(BF)
                rs_copy(way, step, c, stage.at[way, step]).start()
    while to_mix:
        mix(to_mix.pop(0))
    last = half - 1
    for k in range(m):
        for c in (later[0][k],):
            here = pl.ds(c * depth, depth)
            grad_ref[0, :, here] = term[s, :, here].astype(F32)
    for k in range(m):
        for way in range(2):
            c = later[way][k]
            here = pl.ds(c * depth, depth)
            rs_copy(way, last, c, stage.at[way, last]).wait_recv()
            grad_ref[0, :, here] += recv[way, last, :, here].astype(F32)

    for step in range(half):
        for way in range(2):
            for c in ag_parts(way, step):
                ag_copy(way, step, c).wait_send()
    for stage_at, bit, mask, which in w_list:
        w_copy(bit, mask, which).wait_send()
    for step in range(half):
        for way in range(2):
            for c in first[way] if step == 0 else range(m):
                own = step == 0 or (step == 1 and c not in first[way])
                source = term.at[target(way, step)] if own else stage.at[way, step]
                rs_copy(way, step, c, source).wait_send()


def fused(n, m, layer_heads, queries, images, w_key, w_value, key_gain, d_out, img_len, text_start):
    _, text, width = queries.shape
    _, rows, d = images.shape
    _, depth, size = w_key.shape
    half = n // 2
    tokens = n * rows
    copies = 2 * (m - 1)
    anywhere = pl.BlockSpec(memory_space=pl.ANY)
    scalar = pl.BlockSpec(memory_space=pltpu.SMEM)
    vmem = pl.BlockSpec(memory_space=pltpu.VMEM)
    dma = pltpu.SemaphoreType.DMA
    return pl.pallas_call(
        functools.partial(kernel, n, m, layer_heads),
        out_shape=(
            jax.ShapeDtypeStruct((1, text, width), BF),
            jax.ShapeDtypeStruct((1, rows, d), F32),
        ),
        in_specs=[scalar, scalar, vmem] + [anywhere] * 5,
        out_specs=(vmem, vmem),
        scratch_shapes=[
            pltpu.VMEM((n, rows, d), BF),
            pltpu.VMEM((m, depth, size), BF),
            pltpu.VMEM((m, depth, size), BF),
            pltpu.VMEM((text, width), BF),
            pltpu.VMEM((text, width), BF),
            pltpu.VMEM((width // size, tokens, text), BF),
            pltpu.VMEM((n, rows, d), BF),
            pltpu.VMEM((2, half, rows, d), BF),
            pltpu.VMEM((2, half, rows, d), BF),
            pltpu.VMEM((tokens, size), F32),
            pltpu.VMEM((tokens, size), F32),
            pltpu.VMEM((tokens, size), F32),
            pltpu.VMEM((tokens, size), F32),
            dma((5,)),
            dma((2, half, PARTS)),
            dma((2, half, PARTS)),
            dma((copies,)),
            dma((copies,)),
            dma((2, half, m)),
            dma((2, half, m)),
        ],
        compiler_params=pltpu.CompilerParams(
            collective_id=0, has_side_effects=True, vmem_limit_bytes=40 * 1024 * 1024
        ),
    )(img_len, text_start, key_gain, queries, images, w_key, w_value, d_out)


def solution(mesh):
    n, m = mesh.shape["section"], mesh.shape["dp"]

    def local(queries, images, w_key, w_value, key_gain, d_out, img_len, text_start):
        layer_heads = n * w_key.shape[0] // key_gain.shape[0]
        rows = images.shape[1]
        depth, size = w_key.shape[1:]
        heads = queries.shape[2] // size
        fits = (
            rows % 16 == 0 and depth % 128 == 0 and n >= 4 and n % 2 == 0
            and m == 4 and heads % 2 == 0
        )
        form = functools.partial(fused, n, m) if fits else plain
        return form(layer_heads, queries, images, w_key, w_value, key_gain, d_out, img_len, text_start)

    return jax.shard_map(
        local,
        mesh=mesh,
        in_specs=(
            P("section", "dp", None),
            P("dp", "section", None),
            P("section", "dp", None),
            P("section", "dp", None),
            P(),
            P("section", "dp", None),
            P("dp"),
            P("dp"),
        ),
        out_specs=(P("section", "dp", None), P("dp", "section", None)),
        check_vma=False,
    )
```

```python
import functools
import math

import jax
import jax.numpy as jnp
from jax import lax
from jax.experimental import pallas as pl
from jax.experimental.pallas import tpu as pltpu
from jax.sharding import PartitionSpec as P

MESH = pl.DeviceIdType.MESH
W_PARTS = 2
PARTS = 2
BF = jnp.bfloat16
F32 = jnp.float32


def attend(key_raw, value_raw, key_gain, queries, length, start):
    inverse = lax.rsqrt(jnp.mean(key_raw * key_raw, axis=-1, keepdims=True) + 1e-05)
    keys = (key_raw * inverse * key_gain).astype(jnp.bfloat16)
    values = value_raw.astype(jnp.bfloat16)
    head_size = key_gain.shape[-1]
    heads = queries.reshape(queries.shape[0], -1, head_size).astype(jnp.float32)
    scores = jnp.einsum("thd,jd->htj", heads, keys.astype(jnp.float32)) / math.sqrt(head_size)
    usable = jnp.arange(keys.shape[0]) < length
    scores = jnp.where(usable, scores, -1e30)
    scores = scores - jnp.max(scores, axis=-1, keepdims=True)
    expo = jnp.exp(scores)
    probs = (expo / jnp.sum(expo, axis=-1, keepdims=True)).astype(jnp.bfloat16)
    mixed = jnp.einsum("htj,jd->thd", probs.astype(jnp.float32), values.astype(jnp.float32))
    mixed = mixed.reshape(queries.shape[0], -1)
    shown = jnp.arange(queries.shape[0]) >= start
    return jnp.where(shown[:, None], mixed, 0.0)


def plain(layer_heads, queries, images, w_key, w_value, key_gain, d_out, img_len, text_start):
    image_full = lax.all_gather(images[0], "section", axis=0, tiled=True)
    layer = lax.axis_index("section") // layer_heads
    gain = lax.dynamic_index_in_dim(key_gain, layer, 0, keepdims=False)
    key_weight = lax.all_gather(w_key[0], "dp", axis=0, tiled=True)
    value_weight = lax.all_gather(w_value[0], "dp", axis=0, tiled=True)
    key_raw = jnp.dot(image_full, key_weight, preferred_element_type=jnp.float32)
    value_raw = jnp.dot(image_full, value_weight, preferred_element_type=jnp.float32)
    mixed, pull_back = jax.vjp(
        lambda kr, vr: attend(kr, vr, gain, queries[0], img_len[0], text_start[0]), key_raw, value_raw
    )
    d_key, d_value = pull_back(d_out[0].astype(jnp.float32))
    term = jnp.dot(d_key.astype(BF), key_weight.T, preferred_element_type=jnp.float32)
    term = term + jnp.dot(d_value.astype(BF), value_weight.T, preferred_element_type=jnp.float32)
    own = lax.psum_scatter(term.astype(BF), "section", scatter_dimension=0, tiled=True)
    return mixed.astype(BF)[None], own.astype(jnp.float32)[None]


def nt(a, b):
    return lax.dot_general(a, b, (((1,), (1,)), ((), ())), preferred_element_type=F32)


def kernel(
    n, m, layer_heads,
    len_hbm, start_hbm, gain_hbm, q_hbm, img_hbm, wk_hbm, wv_hbm, do_hbm,
    att_out, grad_out,
    att_ref, grad_ref, len_ref, start_ref, gain_ref,
    img, wk, wv, q, do, exact, probs, term, stage, recv, kraw, vraw, dk, dv,
    local_sem, ag_send, ag_recv, w_send, w_recv, rs_send, rs_recv,
):
    half = n // 2
    s = lax.axis_index("section")
    g = lax.axis_index("dp")
    x = lax.rem(s, 2)
    pos = (1 - x) * lax.div(s, 2) + x * (n - 1 - lax.div(s, 2))

    def sec(offset):
        at = lax.rem(pos + offset + n, n)
        hi = lax.div(at, half)
        return (1 - hi) * 2 * at + hi * (2 * (n - 1 - at) + 1)

    def dp_flip(bit):
        return g + bit - 2 * bit * lax.rem(lax.div(g, bit), 2)

    def dp_xor(mask):
        at = g
        for k in range(m.bit_length() - 1):
            if mask & (1 << k):
                at = at + (1 << k) - 2 * (1 << k) * lax.rem(lax.div(g, 1 << k), 2)
        return at

    bits = [1 << k for k in reversed(range(m.bit_length() - 1))]
    right, left = sec(1), sec(-1)
    barrier = pltpu.get_barrier_semaphore()
    for neighbour in (left, right):
        pl.semaphore_signal(barrier, inc=1, device_id={"section": neighbour}, device_id_type=MESH)
    for bit in bits:
        pl.semaphore_signal(barrier, inc=1, device_id={"dp": dp_flip(bit)}, device_id_type=MESH)

    locals_ = [
        pltpu.make_async_copy(img_hbm.at[0], img.at[s], local_sem.at[0]),
        pltpu.make_async_copy(wk_hbm.at[0], wk.at[g], local_sem.at[1]),
        pltpu.make_async_copy(wv_hbm.at[0], wv.at[g], local_sem.at[2]),
        pltpu.make_async_copy(q_hbm.at[0], q, local_sem.at[3]),
        pltpu.make_async_copy(do_hbm.at[0], do, local_sem.at[4]),
        pltpu.make_async_copy(gain_hbm, gain_ref, local_sem.at[5]),
        pltpu.make_async_copy(len_hbm, len_ref, local_sem.at[6]),
        pltpu.make_async_copy(start_hbm, start_ref, local_sem.at[7]),
    ]
    for copy in locals_:
        copy.start()
    pl.semaphore_wait(barrier, 2 + len(bits))

    cols = img.shape[2]
    part = cols // PARTS
    to = (right, left)

    def ag_copy(way, step, c):
        block = sec(-step if way == 0 else step)
        here = pl.ds(c * part, part)
        source = img_hbm.at[0, :, here] if step == 0 else img.at[block, :, here]
        return pltpu.make_async_remote_copy(
            src_ref=source,
            dst_ref=img.at[block, :, here],
            send_sem=ag_send.at[way, step, c],
            recv_sem=ag_recv.at[way, step, c],
            device_id={"section": to[way]},
            device_id_type=MESH,
        )

    def ag_arrival(way, step, c):
        block = sec(-step - 1 if way == 0 else step + 1)
        here = pl.ds(c * part, part)
        return pltpu.make_async_remote_copy(
            src_ref=img.at[block, :, here],
            dst_ref=img.at[block, :, here],
            send_sem=ag_send.at[way, step, c],
            recv_sem=ag_recv.at[way, step, c],
            device_id={"section": to[way]},
            device_id_type=MESH,
        )

    def ag_parts(way, step):
        if step < half - 1:
            return range(PARTS)
        cut = PARTS // 2
        return range(cut) if way == 0 else range(cut, PARTS)

    depth = wk.shape[1]
    cut = depth // W_PARTS
    w_list = []
    held = [0]
    for bit in bits:
        for mask in list(held):
            for which in range(2):
                for c in range(W_PARTS):
                    w_list.append((bit, mask, which, c))
            held.append(mask | bit)
    w_index = {item: k for k, item in enumerate(w_list)}

    def w_copy(bit, mask, which, c):
        k = w_index[(bit, mask, which, c)]
        block = dp_xor(mask)
        here = pl.ds(c * cut, cut)
        full, mine = ((wk, wk_hbm), (wv, wv_hbm))[which]
        return pltpu.make_async_remote_copy(
            src_ref=mine.at[0, here] if mask == 0 else full.at[block, here],
            dst_ref=full.at[block, here],
            send_sem=w_send.at[k],
            recv_sem=w_recv.at[k],
            device_id={"dp": dp_flip(bit)},
            device_id_type=MESH,
        )

    def w_take(bit, mask, which, c):
        k = w_index[(bit, mask, which, c)]
        here = pl.ds(c * cut, cut)
        landed = (wk, wv)[which].at[dp_xor(mask | bit), here]
        pltpu.make_async_remote_copy(
            src_ref=landed,
            dst_ref=landed,
            send_sem=w_send.at[k],
            recv_sem=w_recv.at[k],
            device_id={"dp": dp_flip(bit)},
            device_id_type=MESH,
        ).wait_recv()
        for low in bits:
            if low < bit:
                w_copy(low, mask | bit, which, c).start()

    far, near = bits
    tokens = n * img.shape[1]

    def project(mask, which):
        block = dp_xor(mask)
        columns = pl.ds(pl.multiple_of(block * depth, depth), depth)
        rows = img[:, :, columns].reshape(tokens, depth)
        full, raw = ((wk, kraw), (wv, vraw))[which]
        value = jnp.dot(rows, full[block], preferred_element_type=F32)
        if mask == 0:
            raw[...] = value
        else:
            raw[...] += value

    for c in range(W_PARTS):
        w_copy(far, 0, 0, c).start()
    for c in range(PARTS):
        for way in range(2):
            if c in ag_parts(way, 0):
                ag_copy(way, 0, c).start()
    for which in range(2):
        for c in range(W_PARTS):
            w_copy(near, 0, which, c).start()
    for step in range(1, half):
        for c in range(PARTS):
            for way in range(2):
                if c in ag_parts(way, step - 1):
                    ag_arrival(way, step - 1, c).wait_recv()
                    if c in ag_parts(way, step):
                        ag_copy(way, step, c).start()
        if step == half // 2:
            for c in range(W_PARTS):
                w_copy(far, 0, 0, c).wait_send()
                w_copy(far, 0, 1, c).start()
    for copy in locals_:
        copy.wait()
    for c in range(W_PARTS):
        w_take(far, 0, 0, c)
    for which in range(2):
        for c in range(W_PARTS):
            w_take(near, 0, which, c)
    for c in range(W_PARTS):
        w_take(near, far, 0, c)
    for c in range(W_PARTS - 1):
        w_take(far, 0, 1, c)
    for way in range(2):
        for c in ag_parts(way, half - 1):
            ag_arrival(way, half - 1, c).wait_recv()
    for mask in (0, near, far, far | near):
        project(mask, 0)

    size = kraw.shape[1]
    text = q.shape[0]
    heads = q.shape[1] // size
    layer = lax.div(s, layer_heads)
    gain = gain_ref[pl.ds(layer, 1), :]
    key_raw = kraw[...]
    inverse = lax.rsqrt(jnp.mean(key_raw * key_raw, axis=-1, keepdims=True) + 1e-05)
    keys = (key_raw * inverse * gain).astype(BF)
    usable = lax.broadcasted_iota(jnp.int32, (tokens, text), 0) < len_ref[0]
    shown = lax.broadcasted_iota(jnp.int32, (1, text), 1) >= start_ref[0]
    scale = 1.0 / math.sqrt(size)
    scale2 = scale * math.log2(math.e)

    def forward(h):
        at = pl.ds(h * size, size)
        scores = jnp.where(usable, nt(keys, q[:, at]) * scale2, -1e30)
        expo = jnp.exp2(scores - jnp.max(scores, axis=0, keepdims=True))
        factor = jnp.where(shown, 1.0 / jnp.sum(expo, axis=0, keepdims=True), 0.0)
        p = expo * factor
        half_p = p.astype(BF)
        exact[h] = p
        probs[h] = half_p
        return jnp.dot(half_p, do[:, at], preferred_element_type=F32)

    def backward(h):
        at = pl.ds(h * size, size)
        p = exact[h]
        d_p = nt(values, do[:, at]).astype(BF).astype(F32)
        d_s = (p * (d_p - jnp.sum(p * d_p, axis=0, keepdims=True))).astype(BF)
        return jnp.dot(d_s, q[:, at], preferred_element_type=F32)

    first_heads = heads // 2
    dv[...] = sum(forward(h) for h in range(first_heads))
    w_take(far, 0, 1, W_PARTS - 1)
    dv[...] += sum(forward(h) for h in range(first_heads, heads))
    for mask in (0, near, far):
        project(mask, 1)
    for c in range(W_PARTS):
        w_take(near, far, 1, c)
    project(far | near, 1)
    values = vraw[...].astype(BF)
    dk[...] = sum(backward(h) for h in range(first_heads))
    dk[...] += sum(backward(h) for h in range(first_heads, heads))
    d_keys = (dk[...] * scale).astype(BF).astype(F32) * gain
    d_key = inverse * (d_keys - key_raw * (inverse * inverse) * jnp.mean(d_keys * key_raw, axis=-1, keepdims=True))
    d_key = d_key.astype(BF)
    d_value = dv[...].astype(BF)

    rows = img.shape[1]
    first = (list(range(m // 2)), list(range(m // 2, m)))
    later = (first[1] + first[0], first[0] + first[1])

    def rs_copy(way, step, c, source):
        here = pl.ds(c * depth, depth)
        return pltpu.make_async_remote_copy(
            src_ref=source.at[:, here],
            dst_ref=recv.at[way, step, :, here],
            send_sem=rs_send.at[way, step, c],
            recv_sem=rs_recv.at[way, step, c],
            device_id={"section": to[way]},
            device_id_type=MESH,
        )

    def target(way, step):
        return sec(half - step if way == 0 else step - half)

    order = [c for both in zip(*first) for c in both]
    for c in order:
        here = pl.ds(c * depth, depth)
        value = nt(d_key, wk[c]) + nt(d_value, wv[c])
        term[:, :, here] = value.astype(BF).reshape(n, rows, depth)
        for way in range(2):
            step = 0 if c in first[way] else 1
            if step < half:
                rs_copy(way, step, c, term.at[target(way, step)]).start()

    def mix(h):
        at = pl.ds(h * size, size)
        att_ref[:, at] = lax.dot_general(
            probs[h], values, (((0,), (0,)), ((), ())), preferred_element_type=F32
        ).astype(BF)

    to_mix = list(range(heads))
    for step in range(1, half):
        for k in range(m):
            if to_mix:
                mix(to_mix.pop(0))
            for way in range(2):
                c = later[way][k]
                if step == 1 and c not in first[way]:
                    continue
                here = pl.ds(c * depth, depth)
                rs_copy(way, step - 1, c, stage.at[way, step]).wait_recv()
                total = term[target(way, step), :, here].astype(F32) + recv[way, step - 1, :, here].astype(F32)
                stage[way, step, :, here] = total.astype(BF)
                rs_copy(way, step, c, stage.at[way, step]).start()
    while to_mix:
        mix(to_mix.pop(0))
    att_copy = pltpu.make_async_copy(att_ref, att_out.at[0], local_sem.at[0])
    att_copy.start()
    last = half - 1
    grad_copies = []
    seen = []
    for k in range(m):
        for way in range(2):
            c = later[way][k]
            here = pl.ds(c * depth, depth)
            rs_copy(way, last, c, stage.at[way, last]).wait_recv()
            value = recv[way, last, :, here].astype(F32)
            if c not in seen:
                seen.append(c)
                grad_ref[:, here] = term[s, :, here].astype(F32) + value
            else:
                grad_ref[:, here] += value
                copy = pltpu.make_async_copy(grad_ref.at[:, here], grad_out.at[0, :, here], local_sem.at[1 + c])
                copy.start()
                grad_copies.append(copy)

    att_copy.wait()
    for copy in grad_copies:
        copy.wait()
    for step in range(half):
        for way in range(2):
            for c in ag_parts(way, step):
                ag_copy(way, step, c).wait_send()
    for bit, mask, which, c in w_list:
        if (bit, which) != (far, 0):
            w_copy(bit, mask, which, c).wait_send()
    for step in range(half):
        for way in range(2):
            for c in first[way] if step == 0 else range(m):
                own = step == 0 or (step == 1 and c not in first[way])
                source = term.at[target(way, step)] if own else stage.at[way, step]
                rs_copy(way, step, c, source).wait_send()


def fused(n, m, layer_heads, queries, images, w_key, w_value, key_gain, d_out, img_len, text_start):
    _, text, width = queries.shape
    _, rows, d = images.shape
    _, depth, size = w_key.shape
    half = n // 2
    tokens = n * rows
    copies = 2 * (m - 1) * W_PARTS
    hbm = pl.BlockSpec(memory_space=pl.ANY)
    dma = pltpu.SemaphoreType.DMA
    return pl.pallas_call(
        functools.partial(kernel, n, m, layer_heads),
        out_shape=(
            jax.ShapeDtypeStruct((1, text, width), BF),
            jax.ShapeDtypeStruct((1, rows, d), F32),
        ),
        in_specs=[hbm] * 8,
        out_specs=(hbm, hbm),
        scratch_shapes=[
            pltpu.VMEM((text, width), BF),
            pltpu.VMEM((rows, d), F32),
            pltpu.SMEM(img_len.shape, img_len.dtype),
            pltpu.SMEM(text_start.shape, text_start.dtype),
            pltpu.VMEM(key_gain.shape, key_gain.dtype),
            pltpu.VMEM((n, rows, d), BF),
            pltpu.VMEM((m, depth, size), BF),
            pltpu.VMEM((m, depth, size), BF),
            pltpu.VMEM((text, width), BF),
            pltpu.VMEM((text, width), BF),
            pltpu.VMEM((width // size, tokens, text), F32),
            pltpu.VMEM((width // size, tokens, text), BF),
            pltpu.VMEM((n, rows, d), BF),
            pltpu.VMEM((2, half, rows, d), BF),
            pltpu.VMEM((2, half, rows, d), BF),
            pltpu.VMEM((tokens, size), F32),
            pltpu.VMEM((tokens, size), F32),
            pltpu.VMEM((tokens, size), F32),
            pltpu.VMEM((tokens, size), F32),
            dma((8,)),
            dma((2, half, PARTS)),
            dma((2, half, PARTS)),
            dma((copies,)),
            dma((copies,)),
            dma((2, half, m)),
            dma((2, half, m)),
        ],
        compiler_params=pltpu.CompilerParams(
            collective_id=0, has_side_effects=True, vmem_limit_bytes=63 * 1024 * 1024
        ),
    )(img_len, text_start, key_gain, queries, images, w_key, w_value, d_out)


def solution(mesh):
    n, m = mesh.shape["section"], mesh.shape["dp"]

    def local(queries, images, w_key, w_value, key_gain, d_out, img_len, text_start):
        layer_heads = n * w_key.shape[0] // key_gain.shape[0]
        rows = images.shape[1]
        depth, size = w_key.shape[1:]
        heads = queries.shape[2] // size
        fits = (
            rows % 16 == 0 and depth % 128 == 0 and n >= 4 and n % 2 == 0
            and m == 4 and heads % 2 == 0
        )
        form = functools.partial(fused, n, m) if fits else plain
        return form(layer_heads, queries, images, w_key, w_value, key_gain, d_out, img_len, text_start)

    return jax.shard_map(
        local,
        mesh=mesh,
        in_specs=(
            P("section", "dp", None),
            P("dp", "section", None),
            P("section", "dp", None),
            P("section", "dp", None),
            P(),
            P("section", "dp", None),
            P("dp"),
            P("dp"),
        ),
        out_specs=(P("section", "dp", None), P("dp", "section", None)),
        check_vma=False,
    )
```

```python
import functools
import math

import jax
import jax.numpy as jnp
from jax import lax
from jax.experimental import pallas as pl
from jax.experimental.pallas import tpu as pltpu
from jax.sharding import PartitionSpec as P

MESH = pl.DeviceIdType.MESH
W_PARTS = 2
PARTS = 2
BF = jnp.bfloat16
F32 = jnp.float32


def attend(key_raw, value_raw, key_gain, queries, length, start):
    inverse = lax.rsqrt(jnp.mean(key_raw * key_raw, axis=-1, keepdims=True) + 1e-05)
    keys = (key_raw * inverse * key_gain).astype(jnp.bfloat16)
    values = value_raw.astype(jnp.bfloat16)
    head_size = key_gain.shape[-1]
    heads = queries.reshape(queries.shape[0], -1, head_size).astype(jnp.float32)
    scores = jnp.einsum("thd,jd->htj", heads, keys.astype(jnp.float32)) / math.sqrt(head_size)
    usable = jnp.arange(keys.shape[0]) < length
    scores = jnp.where(usable, scores, -1e30)
    scores = scores - jnp.max(scores, axis=-1, keepdims=True)
    expo = jnp.exp(scores)
    probs = (expo / jnp.sum(expo, axis=-1, keepdims=True)).astype(jnp.bfloat16)
    mixed = jnp.einsum("htj,jd->thd", probs.astype(jnp.float32), values.astype(jnp.float32))
    mixed = mixed.reshape(queries.shape[0], -1)
    shown = jnp.arange(queries.shape[0]) >= start
    return jnp.where(shown[:, None], mixed, 0.0)


def plain(layer_heads, queries, images, w_key, w_value, key_gain, d_out, img_len, text_start):
    image_full = lax.all_gather(images[0], "section", axis=0, tiled=True)
    layer = lax.axis_index("section") // layer_heads
    gain = lax.dynamic_index_in_dim(key_gain, layer, 0, keepdims=False)
    key_weight = lax.all_gather(w_key[0], "dp", axis=0, tiled=True)
    value_weight = lax.all_gather(w_value[0], "dp", axis=0, tiled=True)
    key_raw = jnp.dot(image_full, key_weight, preferred_element_type=jnp.float32)
    value_raw = jnp.dot(image_full, value_weight, preferred_element_type=jnp.float32)
    mixed, pull_back = jax.vjp(
        lambda kr, vr: attend(kr, vr, gain, queries[0], img_len[0], text_start[0]), key_raw, value_raw
    )
    d_key, d_value = pull_back(d_out[0].astype(jnp.float32))
    term = jnp.dot(d_key.astype(BF), key_weight.T, preferred_element_type=jnp.float32)
    term = term + jnp.dot(d_value.astype(BF), value_weight.T, preferred_element_type=jnp.float32)
    own = lax.psum_scatter(term.astype(BF), "section", scatter_dimension=0, tiled=True)
    return mixed.astype(BF)[None], own.astype(jnp.float32)[None]


def nt(a, b):
    return lax.dot_general(a, b, (((1,), (1,)), ((), ())), preferred_element_type=F32)


def kernel(
    n, m, layer_heads,
    len_hbm, start_hbm, gain_hbm, q_hbm, img_hbm, wk_hbm, wv_hbm, do_hbm,
    att_ref, grad_ref,
    len_ref, start_ref, gain_ref,
    img, wk, wv, q, do, exact, probs, term, stage, recv, kraw, vraw, dk, dv,
    local_sem, ag_send, ag_recv, w_send, w_recv, rs_send, rs_recv,
):
    half = n // 2
    s = lax.axis_index("section")
    g = lax.axis_index("dp")
    x = lax.rem(s, 2)
    pos = (1 - x) * lax.div(s, 2) + x * (n - 1 - lax.div(s, 2))

    def sec(offset):
        at = lax.rem(pos + offset + n, n)
        hi = lax.div(at, half)
        return (1 - hi) * 2 * at + hi * (2 * (n - 1 - at) + 1)

    def dp_flip(bit):
        return g + bit - 2 * bit * lax.rem(lax.div(g, bit), 2)

    def dp_xor(mask):
        at = g
        for k in range(m.bit_length() - 1):
            if mask & (1 << k):
                at = at + (1 << k) - 2 * (1 << k) * lax.rem(lax.div(g, 1 << k), 2)
        return at

    bits = [1 << k for k in reversed(range(m.bit_length() - 1))]
    right, left = sec(1), sec(-1)
    barrier = pltpu.get_barrier_semaphore()
    for neighbour in (left, right):
        pl.semaphore_signal(barrier, inc=1, device_id={"section": neighbour}, device_id_type=MESH)
    for bit in bits:
        pl.semaphore_signal(barrier, inc=1, device_id={"dp": dp_flip(bit)}, device_id_type=MESH)

    locals_ = [
        pltpu.make_async_copy(img_hbm.at[0], img.at[s], local_sem.at[0]),
        pltpu.make_async_copy(wk_hbm.at[0], wk.at[g], local_sem.at[1]),
        pltpu.make_async_copy(wv_hbm.at[0], wv.at[g], local_sem.at[2]),
        pltpu.make_async_copy(q_hbm.at[0], q, local_sem.at[3]),
        pltpu.make_async_copy(do_hbm.at[0], do, local_sem.at[4]),
        pltpu.make_async_copy(gain_hbm, gain_ref, local_sem.at[5]),
        pltpu.make_async_copy(len_hbm, len_ref, local_sem.at[6]),
        pltpu.make_async_copy(start_hbm, start_ref, local_sem.at[7]),
    ]
    for copy in locals_:
        copy.start()
    pl.semaphore_wait(barrier, 2 + len(bits))

    cols = img.shape[2]
    part = cols // PARTS
    to = (right, left)

    def ag_copy(way, step, c):
        block = sec(-step if way == 0 else step)
        here = pl.ds(c * part, part)
        source = img_hbm.at[0, :, here] if step == 0 else img.at[block, :, here]
        return pltpu.make_async_remote_copy(
            src_ref=source,
            dst_ref=img.at[block, :, here],
            send_sem=ag_send.at[way, step, c],
            recv_sem=ag_recv.at[way, step, c],
            device_id={"section": to[way]},
            device_id_type=MESH,
        )

    def ag_arrival(way, step, c):
        block = sec(-step - 1 if way == 0 else step + 1)
        here = pl.ds(c * part, part)
        return pltpu.make_async_remote_copy(
            src_ref=img.at[block, :, here],
            dst_ref=img.at[block, :, here],
            send_sem=ag_send.at[way, step, c],
            recv_sem=ag_recv.at[way, step, c],
            device_id={"section": to[way]},
            device_id_type=MESH,
        )

    def ag_parts(way, step):
        if step < half - 1:
            return range(PARTS)
        cut = PARTS // 2
        return range(cut) if way == 0 else range(cut, PARTS)

    depth = wk.shape[1]
    cut = depth // W_PARTS
    w_list = []
    held = [0]
    for bit in bits:
        for mask in list(held):
            for which in range(2):
                for c in range(W_PARTS):
                    w_list.append((bit, mask, which, c))
            held.append(mask | bit)
    w_index = {item: k for k, item in enumerate(w_list)}

    def w_copy(bit, mask, which, c):
        k = w_index[(bit, mask, which, c)]
        block = dp_xor(mask)
        here = pl.ds(c * cut, cut)
        full, mine = ((wk, wk_hbm), (wv, wv_hbm))[which]
        return pltpu.make_async_remote_copy(
            src_ref=mine.at[0, here] if mask == 0 else full.at[block, here],
            dst_ref=full.at[block, here],
            send_sem=w_send.at[k],
            recv_sem=w_recv.at[k],
            device_id={"dp": dp_flip(bit)},
            device_id_type=MESH,
        )

    def w_take(bit, mask, which, c):
        k = w_index[(bit, mask, which, c)]
        here = pl.ds(c * cut, cut)
        landed = (wk, wv)[which].at[dp_xor(mask | bit), here]
        pltpu.make_async_remote_copy(
            src_ref=landed,
            dst_ref=landed,
            send_sem=w_send.at[k],
            recv_sem=w_recv.at[k],
            device_id={"dp": dp_flip(bit)},
            device_id_type=MESH,
        ).wait_recv()
        for low in bits:
            if low < bit:
                w_copy(low, mask | bit, which, c).start()

    far, near = bits
    tokens = n * img.shape[1]

    def project(mask, which):
        block = dp_xor(mask)
        columns = pl.ds(pl.multiple_of(block * depth, depth), depth)
        rows = img[:, :, columns].reshape(tokens, depth)
        full, raw = ((wk, kraw), (wv, vraw))[which]
        value = jnp.dot(rows, full[block], preferred_element_type=F32)
        if mask == 0:
            raw[...] = value
        else:
            raw[...] += value

    for c in range(W_PARTS):
        w_copy(far, 0, 0, c).start()
    for c in range(PARTS):
        for way in range(2):
            if c in ag_parts(way, 0):
                ag_copy(way, 0, c).start()
    for which in range(2):
        for c in range(W_PARTS):
            w_copy(near, 0, which, c).start()
    for step in range(1, half):
        for c in range(PARTS):
            for way in range(2):
                if c in ag_parts(way, step - 1):
                    ag_arrival(way, step - 1, c).wait_recv()
                    if c in ag_parts(way, step):
                        ag_copy(way, step, c).start()
        if step <= W_PARTS:
            w_copy(far, 0, 1, step - 1).start()
    for copy in locals_:
        copy.wait()
    for c in range(W_PARTS):
        w_take(far, 0, 0, c)
    for which in range(2):
        for c in range(W_PARTS):
            w_take(near, 0, which, c)
    for c in range(W_PARTS):
        w_take(near, far, 0, c)
    for c in range(W_PARTS - 1):
        w_take(far, 0, 1, c)
    for way in range(2):
        for c in ag_parts(way, half - 1):
            ag_arrival(way, half - 1, c).wait_recv()
    for mask in (0, near, far, far | near):
        project(mask, 0)

    size = kraw.shape[1]
    text = q.shape[0]
    heads = q.shape[1] // size
    layer = lax.div(s, layer_heads)
    gain = gain_ref[pl.ds(layer, 1), :]
    key_raw = kraw[...]
    inverse = lax.rsqrt(jnp.mean(key_raw * key_raw, axis=-1, keepdims=True) + 1e-05)
    keys = (key_raw * inverse * gain).astype(BF)
    usable = lax.broadcasted_iota(jnp.int32, (tokens, text), 0) < len_ref[0]
    shown = lax.broadcasted_iota(jnp.int32, (1, text), 1) >= start_ref[0]
    scale = 1.0 / math.sqrt(size)
    scale2 = scale * math.log2(math.e)

    def forward(h):
        at = pl.ds(h * size, size)
        scores = jnp.where(usable, nt(keys, q[:, at]) * scale2, -1e30)
        expo = jnp.exp2(scores - jnp.max(scores, axis=0, keepdims=True))
        factor = jnp.where(shown, 1.0 / jnp.sum(expo, axis=0, keepdims=True), 0.0)
        p = expo * factor
        half_p = p.astype(BF)
        exact[h] = p
        probs[h] = half_p
        return jnp.dot(half_p, do[:, at], preferred_element_type=F32)

    def backward(h):
        at = pl.ds(h * size, size)
        p = exact[h]
        d_p = nt(values, do[:, at]).astype(BF).astype(F32)
        d_s = (p * (d_p - jnp.sum(p * d_p, axis=0, keepdims=True))).astype(BF)
        return jnp.dot(d_s, q[:, at], preferred_element_type=F32)

    first_heads = heads // 2
    dv[...] = sum(forward(h) for h in range(first_heads))
    w_take(far, 0, 1, W_PARTS - 1)
    dv[...] += sum(forward(h) for h in range(first_heads, heads))
    for mask in (0, near, far):
        project(mask, 1)
    for c in range(W_PARTS):
        w_take(near, far, 1, c)
    project(far | near, 1)
    values = vraw[...].astype(BF)
    dk[...] = sum(backward(h) for h in range(first_heads))
    dk[...] += sum(backward(h) for h in range(first_heads, heads))
    d_keys = (dk[...] * scale).astype(BF).astype(F32) * gain
    d_key = inverse * (d_keys - key_raw * (inverse * inverse) * jnp.mean(d_keys * key_raw, axis=-1, keepdims=True))
    d_key = d_key.astype(BF)
    d_value = dv[...].astype(BF)

    rows = img.shape[1]
    first = (list(range(m // 2)), list(range(m // 2, m)))
    later = (first[1] + first[0], first[0] + first[1])

    def rs_copy(way, step, c, source):
        here = pl.ds(c * depth, depth)
        return pltpu.make_async_remote_copy(
            src_ref=source.at[:, here],
            dst_ref=recv.at[way, step, :, here],
            send_sem=rs_send.at[way, step, c],
            recv_sem=rs_recv.at[way, step, c],
            device_id={"section": to[way]},
            device_id_type=MESH,
        )

    def target(way, step):
        return sec(half - step if way == 0 else step - half)

    order = [c for both in zip(*first) for c in both]
    for c in order:
        here = pl.ds(c * depth, depth)
        value = nt(d_key, wk[c]) + nt(d_value, wv[c])
        term[:, :, here] = value.astype(BF).reshape(n, rows, depth)
        for way in range(2):
            step = 0 if c in first[way] else 1
            if step < half:
                rs_copy(way, step, c, term.at[target(way, step)]).start()

    def mix(h):
        at = pl.ds(h * size, size)
        att_ref[0, :, at] = lax.dot_general(
            probs[h], values, (((0,), (0,)), ((), ())), preferred_element_type=F32
        ).astype(BF)

    to_mix = list(range(heads))
    for step in range(1, half):
        for k in range(m):
            if to_mix:
                mix(to_mix.pop(0))
            for way in range(2):
                c = later[way][k]
                if step == 1 and c not in first[way]:
                    continue
                here = pl.ds(c * depth, depth)
                rs_copy(way, step - 1, c, stage.at[way, step]).wait_recv()
                total = term[target(way, step), :, here].astype(F32) + recv[way, step - 1, :, here].astype(F32)
                stage[way, step, :, here] = total.astype(BF)
                rs_copy(way, step, c, stage.at[way, step]).start()
    while to_mix:
        mix(to_mix.pop(0))
    last = half - 1
    seen = []
    for k in range(m):
        for way in range(2):
            c = later[way][k]
            here = pl.ds(c * depth, depth)
            rs_copy(way, last, c, stage.at[way, last]).wait_recv()
            value = recv[way, last, :, here].astype(F32)
            if c not in seen:
                seen.append(c)
                grad_ref[0, :, here] = term[s, :, here].astype(F32) + value
            else:
                grad_ref[0, :, here] += value

    for step in range(half):
        for way in range(2):
            for c in ag_parts(way, step):
                ag_copy(way, step, c).wait_send()
    for item in w_list:
        w_copy(*item).wait_send()
    for step in range(half):
        for way in range(2):
            for c in first[way] if step == 0 else range(m):
                own = step == 0 or (step == 1 and c not in first[way])
                source = term.at[target(way, step)] if own else stage.at[way, step]
                rs_copy(way, step, c, source).wait_send()


def fused(n, m, layer_heads, queries, images, w_key, w_value, key_gain, d_out, img_len, text_start):
    _, text, width = queries.shape
    _, rows, d = images.shape
    _, depth, size = w_key.shape
    half = n // 2
    tokens = n * rows
    copies = 2 * (m - 1) * W_PARTS
    hbm = pl.BlockSpec(memory_space=pl.ANY)
    dma = pltpu.SemaphoreType.DMA
    return pl.pallas_call(
        functools.partial(kernel, n, m, layer_heads),
        out_shape=(
            pltpu.VMEM((1, text, width), BF),
            pltpu.VMEM((1, rows, d), F32),
        ),
        in_specs=[hbm] * 8,
        out_specs=(pl.BlockSpec(memory_space=pltpu.VMEM),) * 2,
        scratch_shapes=[
            pltpu.SMEM(img_len.shape, img_len.dtype),
            pltpu.SMEM(text_start.shape, text_start.dtype),
            pltpu.VMEM(key_gain.shape, key_gain.dtype),
            pltpu.VMEM((n, rows, d), BF),
            pltpu.VMEM((m, depth, size), BF),
            pltpu.VMEM((m, depth, size), BF),
            pltpu.VMEM((text, width), BF),
            pltpu.VMEM((text, width), BF),
            pltpu.VMEM((width // size, tokens, text), F32),
            pltpu.VMEM((width // size, tokens, text), BF),
            pltpu.VMEM((n, rows, d), BF),
            pltpu.VMEM((2, half, rows, d), BF),
            pltpu.VMEM((2, half, rows, d), BF),
            pltpu.VMEM((tokens, size), F32),
            pltpu.VMEM((tokens, size), F32),
            pltpu.VMEM((tokens, size), F32),
            pltpu.VMEM((tokens, size), F32),
            dma((8,)),
            dma((2, half, PARTS)),
            dma((2, half, PARTS)),
            dma((copies,)),
            dma((copies,)),
            dma((2, half, m)),
            dma((2, half, m)),
        ],
        compiler_params=pltpu.CompilerParams(
            collective_id=0, has_side_effects=True, vmem_limit_bytes=60 * 1024 * 1024
        ),
    )(img_len, text_start, key_gain, queries, images, w_key, w_value, d_out)


def solution(mesh):
    n, m = mesh.shape["section"], mesh.shape["dp"]

    def local(queries, images, w_key, w_value, key_gain, d_out, img_len, text_start):
        layer_heads = n * w_key.shape[0] // key_gain.shape[0]
        rows = images.shape[1]
        depth, size = w_key.shape[1:]
        heads = queries.shape[2] // size
        fits = (
            rows % 16 == 0 and depth % 128 == 0 and n >= 4 and n % 2 == 0
            and m == 4 and heads % 2 == 0
        )
        form = functools.partial(fused, n, m) if fits else plain
        return form(layer_heads, queries, images, w_key, w_value, key_gain, d_out, img_len, text_start)

    return jax.shard_map(
        local,
        mesh=mesh,
        in_specs=(
            P("section", "dp", None),
            P("dp", "section", None),
            P("section", "dp", None),
            P("section", "dp", None),
            P(),
            P("section", "dp", None),
            P("dp"),
            P("dp"),
        ),
        out_specs=(P("section", "dp", None), P("dp", "section", None)),
        check_vma=False,
    )
```

```python
import functools
import math

import jax
import jax.numpy as jnp
from jax import lax
from jax.experimental import pallas as pl
from jax.experimental.pallas import tpu as pltpu
from jax.sharding import PartitionSpec as P

MESH = pl.DeviceIdType.MESH
W_PARTS = 2
PARTS = 2
BF = jnp.bfloat16
F32 = jnp.float32


def attend(key_raw, value_raw, key_gain, queries, length, start):
    inverse = lax.rsqrt(jnp.mean(key_raw * key_raw, axis=-1, keepdims=True) + 1e-05)
    keys = (key_raw * inverse * key_gain).astype(jnp.bfloat16)
    values = value_raw.astype(jnp.bfloat16)
    head_size = key_gain.shape[-1]
    heads = queries.reshape(queries.shape[0], -1, head_size).astype(jnp.float32)
    scores = jnp.einsum("thd,jd->htj", heads, keys.astype(jnp.float32)) / math.sqrt(head_size)
    usable = jnp.arange(keys.shape[0]) < length
    scores = jnp.where(usable, scores, -1e30)
    scores = scores - jnp.max(scores, axis=-1, keepdims=True)
    expo = jnp.exp(scores)
    probs = (expo / jnp.sum(expo, axis=-1, keepdims=True)).astype(jnp.bfloat16)
    mixed = jnp.einsum("htj,jd->thd", probs.astype(jnp.float32), values.astype(jnp.float32))
    mixed = mixed.reshape(queries.shape[0], -1)
    shown = jnp.arange(queries.shape[0]) >= start
    return jnp.where(shown[:, None], mixed, 0.0)


def plain(layer_heads, queries, images, w_key, w_value, key_gain, d_out, img_len, text_start):
    image_full = lax.all_gather(images[0], "section", axis=0, tiled=True)
    layer = lax.axis_index("section") // layer_heads
    gain = lax.dynamic_index_in_dim(key_gain, layer, 0, keepdims=False)
    key_weight = lax.all_gather(w_key[0], "dp", axis=0, tiled=True)
    value_weight = lax.all_gather(w_value[0], "dp", axis=0, tiled=True)
    key_raw = jnp.dot(image_full, key_weight, preferred_element_type=jnp.float32)
    value_raw = jnp.dot(image_full, value_weight, preferred_element_type=jnp.float32)
    mixed, pull_back = jax.vjp(
        lambda kr, vr: attend(kr, vr, gain, queries[0], img_len[0], text_start[0]), key_raw, value_raw
    )
    d_key, d_value = pull_back(d_out[0].astype(jnp.float32))
    term = jnp.dot(d_key.astype(BF), key_weight.T, preferred_element_type=jnp.float32)
    term = term + jnp.dot(d_value.astype(BF), value_weight.T, preferred_element_type=jnp.float32)
    own = lax.psum_scatter(term.astype(BF), "section", scatter_dimension=0, tiled=True)
    return mixed.astype(BF)[None], own.astype(jnp.float32)[None]


def nt(a, b):
    return lax.dot_general(a, b, (((1,), (1,)), ((), ())), preferred_element_type=F32)


def kernel(
    n, m, layer_heads,
    len_hbm, start_hbm, gain_hbm, q_hbm, img_hbm, wk_hbm, wv_hbm, do_hbm,
    att_ref, grad_ref,
    len_ref, start_ref, gain_ref,
    img, wk, wv, q, do, exact, probs, term, stage, recv, kraw, vraw, dk, dv,
    local_sem, ag_send, ag_recv, w_send, w_recv, rs_send, rs_recv,
):
    half = n // 2
    s = lax.axis_index("section")
    g = lax.axis_index("dp")
    x = lax.rem(s, 2)
    pos = (1 - x) * lax.div(s, 2) + x * (n - 1 - lax.div(s, 2))

    def sec(offset):
        at = lax.rem(pos + offset + n, n)
        hi = lax.div(at, half)
        return (1 - hi) * 2 * at + hi * (2 * (n - 1 - at) + 1)

    def dp_flip(bit):
        return g + bit - 2 * bit * lax.rem(lax.div(g, bit), 2)

    def dp_xor(mask):
        at = g
        for k in range(m.bit_length() - 1):
            if mask & (1 << k):
                at = at + (1 << k) - 2 * (1 << k) * lax.rem(lax.div(g, 1 << k), 2)
        return at

    bits = [1 << k for k in reversed(range(m.bit_length() - 1))]
    right, left = sec(1), sec(-1)
    barrier = pltpu.get_barrier_semaphore()
    for neighbour in (left, right):
        pl.semaphore_signal(barrier, inc=1, device_id={"section": neighbour}, device_id_type=MESH)
    for bit in bits:
        pl.semaphore_signal(barrier, inc=1, device_id={"dp": dp_flip(bit)}, device_id_type=MESH)

    locals_ = [
        pltpu.make_async_copy(img_hbm.at[0], img.at[s], local_sem.at[0]),
        pltpu.make_async_copy(wk_hbm.at[0], wk.at[g], local_sem.at[1]),
        pltpu.make_async_copy(wv_hbm.at[0], wv.at[g], local_sem.at[2]),
        pltpu.make_async_copy(q_hbm.at[0], q, local_sem.at[3]),
        pltpu.make_async_copy(do_hbm.at[0], do, local_sem.at[4]),
        pltpu.make_async_copy(gain_hbm, gain_ref, local_sem.at[5]),
        pltpu.make_async_copy(len_hbm, len_ref, local_sem.at[6]),
        pltpu.make_async_copy(start_hbm, start_ref, local_sem.at[7]),
    ]
    for copy in locals_:
        copy.start()
    pl.semaphore_wait(barrier, 2 + len(bits))

    cols = img.shape[2]
    part = cols // PARTS
    to = (right, left)

    def ag_copy(way, step, c):
        block = sec(-step if way == 0 else step)
        here = pl.ds(c * part, part)
        source = img_hbm.at[0, :, here] if step == 0 else img.at[block, :, here]
        return pltpu.make_async_remote_copy(
            src_ref=source,
            dst_ref=img.at[block, :, here],
            send_sem=ag_send.at[way, step, c],
            recv_sem=ag_recv.at[way, step, c],
            device_id={"section": to[way]},
            device_id_type=MESH,
        )

    def ag_arrival(way, step, c):
        block = sec(-step - 1 if way == 0 else step + 1)
        here = pl.ds(c * part, part)
        return pltpu.make_async_remote_copy(
            src_ref=img.at[block, :, here],
            dst_ref=img.at[block, :, here],
            send_sem=ag_send.at[way, step, c],
            recv_sem=ag_recv.at[way, step, c],
            device_id={"section": to[way]},
            device_id_type=MESH,
        )

    def ag_parts(way, step):
        if step < half - 1:
            return range(PARTS)
        cut = PARTS // 2
        return range(cut) if way == 0 else range(cut, PARTS)

    depth = wk.shape[1]
    cut = depth // W_PARTS
    w_list = []
    held = [0]
    for bit in bits:
        for mask in list(held):
            for which in range(2):
                for c in range(W_PARTS):
                    w_list.append((bit, mask, which, c))
            held.append(mask | bit)
    w_index = {item: k for k, item in enumerate(w_list)}

    def w_copy(bit, mask, which, c):
        k = w_index[(bit, mask, which, c)]
        block = dp_xor(mask)
        here = pl.ds(c * cut, cut)
        full, mine = ((wk, wk_hbm), (wv, wv_hbm))[which]
        return pltpu.make_async_remote_copy(
            src_ref=mine.at[0, here] if mask == 0 else full.at[block, here],
            dst_ref=full.at[block, here],
            send_sem=w_send.at[k],
            recv_sem=w_recv.at[k],
            device_id={"dp": dp_flip(bit)},
            device_id_type=MESH,
        )

    def w_take(bit, mask, which, c):
        k = w_index[(bit, mask, which, c)]
        here = pl.ds(c * cut, cut)
        landed = (wk, wv)[which].at[dp_xor(mask | bit), here]
        pltpu.make_async_remote_copy(
            src_ref=landed,
            dst_ref=landed,
            send_sem=w_send.at[k],
            recv_sem=w_recv.at[k],
            device_id={"dp": dp_flip(bit)},
            device_id_type=MESH,
        ).wait_recv()
        for low in bits:
            if low < bit:
                w_copy(low, mask | bit, which, c).start()

    far, near = bits
    tokens = n * img.shape[1]

    def project(mask, which=None):
        block = dp_xor(mask)
        columns = pl.ds(pl.multiple_of(block * depth, depth), depth)
        rows = img[:, :, columns].reshape(tokens, depth)
        if which is None:
            weight = jnp.concatenate([wk[block], wv[block]], axis=1)
            return jnp.dot(rows, weight, preferred_element_type=F32)
        return jnp.dot(rows, (wk, wv)[which][block], preferred_element_type=F32)

    for c in range(W_PARTS):
        w_copy(far, 0, 0, c).start()
    for c in range(PARTS):
        for way in range(2):
            if c in ag_parts(way, 0):
                ag_copy(way, 0, c).start()
    for which in range(2):
        for c in range(W_PARTS):
            w_copy(near, 0, which, c).start()
    for step in range(1, half):
        for c in range(PARTS):
            for way in range(2):
                if c in ag_parts(way, step - 1):
                    ag_arrival(way, step - 1, c).wait_recv()
                    if c in ag_parts(way, step):
                        ag_copy(way, step, c).start()
        if step <= W_PARTS:
            w_copy(far, 0, 1, step - 1).start()
    for copy in locals_:
        copy.wait()
    for c in range(W_PARTS):
        w_take(far, 0, 0, c)
    for which in range(2):
        for c in range(W_PARTS):
            w_take(near, 0, which, c)
    for c in range(W_PARTS):
        w_take(near, far, 0, c)
    for c in range(W_PARTS - 1):
        w_take(far, 0, 1, c)
    for way in range(2):
        for c in ag_parts(way, half - 1):
            ag_arrival(way, half - 1, c).wait_recv()
    both = project(0) + project(near)
    w_take(far, 0, 1, W_PARTS - 1)
    both = both + project(far)

    size = kraw.shape[1]
    kraw[...] = both[:, :size] + project(far | near, 0)
    vraw[...] = both[:, size:]
    text = q.shape[0]
    heads = q.shape[1] // size
    layer = lax.div(s, layer_heads)
    gain = gain_ref[pl.ds(layer, 1), :]
    key_raw = kraw[...]
    inverse = lax.rsqrt(jnp.mean(key_raw * key_raw, axis=-1, keepdims=True) + 1e-05)
    keys = (key_raw * inverse * gain).astype(BF)
    usable = lax.broadcasted_iota(jnp.int32, (tokens, text), 0) < len_ref[0]
    shown = lax.broadcasted_iota(jnp.int32, (1, text), 1) >= start_ref[0]
    scale = 1.0 / math.sqrt(size)
    scale2 = scale * math.log2(math.e)

    def forward(h):
        at = pl.ds(h * size, size)
        scores = jnp.where(usable, nt(keys, q[:, at]) * scale2, -1e30)
        expo = jnp.exp2(scores - jnp.max(scores, axis=0, keepdims=True))
        factor = jnp.where(shown, 1.0 / jnp.sum(expo, axis=0, keepdims=True), 0.0)
        p = expo * factor
        half_p = p.astype(BF)
        exact[h] = p
        probs[h] = half_p
        return jnp.dot(half_p, do[:, at], preferred_element_type=F32)

    def backward(h):
        at = pl.ds(h * size, size)
        p = exact[h]
        d_p = nt(values, do[:, at]).astype(BF).astype(F32)
        d_s = (p * (d_p - jnp.sum(p * d_p, axis=0, keepdims=True))).astype(BF)
        return jnp.dot(d_s, q[:, at], preferred_element_type=F32)

    first_heads = heads // 2
    dv[...] = sum(forward(h) for h in range(first_heads))
    dv[...] += sum(forward(h) for h in range(first_heads, heads))
    for c in range(W_PARTS):
        w_take(near, far, 1, c)
    values = (vraw[...] + project(far | near, 1)).astype(BF)
    dk[...] = sum(backward(h) for h in range(first_heads))
    dk[...] += sum(backward(h) for h in range(first_heads, heads))
    d_keys = (dk[...] * scale).astype(BF).astype(F32) * gain
    d_key = inverse * (d_keys - key_raw * (inverse * inverse) * jnp.mean(d_keys * key_raw, axis=-1, keepdims=True))
    d_both = jnp.concatenate([d_key.astype(BF), dv[...].astype(BF)], axis=1)

    rows = img.shape[1]
    first = (list(range(m // 2)), list(range(m // 2, m)))
    later = (first[1] + first[0], first[0] + first[1])

    def rs_copy(way, step, c, source):
        here = pl.ds(c * depth, depth)
        return pltpu.make_async_remote_copy(
            src_ref=source.at[:, here],
            dst_ref=recv.at[way, step, :, here],
            send_sem=rs_send.at[way, step, c],
            recv_sem=rs_recv.at[way, step, c],
            device_id={"section": to[way]},
            device_id_type=MESH,
        )

    def target(way, step):
        return sec(half - step if way == 0 else step - half)

    order = [c for both in zip(*first) for c in both]
    for c in order:
        here = pl.ds(c * depth, depth)
        value = nt(d_both, jnp.concatenate([wk[c], wv[c]], axis=1))
        term[:, :, here] = value.astype(BF).reshape(n, rows, depth)
        for way in range(2):
            step = 0 if c in first[way] else 1
            if step < half:
                rs_copy(way, step, c, term.at[target(way, step)]).start()

    def mix(h):
        at = pl.ds(h * size, size)
        att_ref[0, :, at] = lax.dot_general(
            probs[h], values, (((0,), (0,)), ((), ())), preferred_element_type=F32
        ).astype(BF)

    to_mix = list(range(heads))
    for step in range(1, half):
        for k in range(m):
            if to_mix:
                mix(to_mix.pop(0))
            for way in range(2):
                c = later[way][k]
                if step == 1 and c not in first[way]:
                    continue
                here = pl.ds(c * depth, depth)
                rs_copy(way, step - 1, c, stage.at[way, step]).wait_recv()
                total = term[target(way, step), :, here].astype(F32) + recv[way, step - 1, :, here].astype(F32)
                stage[way, step, :, here] = total.astype(BF)
                rs_copy(way, step, c, stage.at[way, step]).start()
    while to_mix:
        mix(to_mix.pop(0))
    last = half - 1
    seen = []
    for k in range(m):
        for way in range(2):
            c = later[way][k]
            here = pl.ds(c * depth, depth)
            rs_copy(way, last, c, stage.at[way, last]).wait_recv()
            value = recv[way, last, :, here].astype(F32)
            if c not in seen:
                seen.append(c)
                grad_ref[0, :, here] = term[s, :, here].astype(F32) + value
            else:
                grad_ref[0, :, here] += value

    for step in range(half):
        for way in range(2):
            for c in ag_parts(way, step):
                ag_copy(way, step, c).wait_send()
    for item in w_list:
        w_copy(*item).wait_send()
    for step in range(half):
        for way in range(2):
            for c in first[way] if step == 0 else range(m):
                own = step == 0 or (step == 1 and c not in first[way])
                source = term.at[target(way, step)] if own else stage.at[way, step]
                rs_copy(way, step, c, source).wait_send()


def fused(n, m, layer_heads, queries, images, w_key, w_value, key_gain, d_out, img_len, text_start):
    _, text, width = queries.shape
    _, rows, d = images.shape
    _, depth, size = w_key.shape
    half = n // 2
    tokens = n * rows
    copies = 2 * (m - 1) * W_PARTS
    hbm = pl.BlockSpec(memory_space=pl.ANY)
    dma = pltpu.SemaphoreType.DMA
    return pl.pallas_call(
        functools.partial(kernel, n, m, layer_heads),
        out_shape=(
            pltpu.VMEM((1, text, width), BF),
            pltpu.VMEM((1, rows, d), F32),
        ),
        in_specs=[hbm] * 8,
        out_specs=(pl.BlockSpec(memory_space=pltpu.VMEM),) * 2,
        scratch_shapes=[
            pltpu.SMEM(img_len.shape, img_len.dtype),
            pltpu.SMEM(text_start.shape, text_start.dtype),
            pltpu.VMEM(key_gain.shape, key_gain.dtype),
            pltpu.VMEM((n, rows, d), BF),
            pltpu.VMEM((m, depth, size), BF),
            pltpu.VMEM((m, depth, size), BF),
            pltpu.VMEM((text, width), BF),
            pltpu.VMEM((text, width), BF),
            pltpu.VMEM((width // size, tokens, text), F32),
            pltpu.VMEM((width // size, tokens, text), BF),
            pltpu.VMEM((n, rows, d), BF),
            pltpu.VMEM((2, half, rows, d), BF),
            pltpu.VMEM((2, half, rows, d), BF),
            pltpu.VMEM((tokens, size), F32),
            pltpu.VMEM((tokens, size), F32),
            pltpu.VMEM((tokens, size), F32),
            pltpu.VMEM((tokens, size), F32),
            dma((8,)),
            dma((2, half, PARTS)),
            dma((2, half, PARTS)),
            dma((copies,)),
            dma((copies,)),
            dma((2, half, m)),
            dma((2, half, m)),
        ],
        compiler_params=pltpu.CompilerParams(
            collective_id=0, has_side_effects=True, vmem_limit_bytes=60 * 1024 * 1024
        ),
    )(img_len, text_start, key_gain, queries, images, w_key, w_value, d_out)


def solution(mesh):
    n, m = mesh.shape["section"], mesh.shape["dp"]

    def local(queries, images, w_key, w_value, key_gain, d_out, img_len, text_start):
        layer_heads = n * w_key.shape[0] // key_gain.shape[0]
        rows = images.shape[1]
        depth, size = w_key.shape[1:]
        heads = queries.shape[2] // size
        fits = (
            rows % 16 == 0 and depth % 128 == 0 and n >= 4 and n % 2 == 0
            and m == 4 and heads % 2 == 0
        )
        form = functools.partial(fused, n, m) if fits else plain
        return form(layer_heads, queries, images, w_key, w_value, key_gain, d_out, img_len, text_start)

    return jax.shard_map(
        local,
        mesh=mesh,
        in_specs=(
            P("section", "dp", None),
            P("dp", "section", None),
            P("section", "dp", None),
            P("section", "dp", None),
            P(),
            P("section", "dp", None),
            P("dp"),
            P("dp"),
        ),
        out_specs=(P("section", "dp", None), P("dp", "section", None)),
        check_vma=False,
    )
```

```python
import functools
import math

import jax
import jax.numpy as jnp
from jax import lax
from jax.experimental import pallas as pl
from jax.experimental.pallas import tpu as pltpu
from jax.sharding import PartitionSpec as P

MESH = pl.DeviceIdType.MESH
W_PARTS = 2
PARTS = 4
BF = jnp.bfloat16
F32 = jnp.float32


def attend(key_raw, value_raw, key_gain, queries, length, start):
    inverse = lax.rsqrt(jnp.mean(key_raw * key_raw, axis=-1, keepdims=True) + 1e-05)
    keys = (key_raw * inverse * key_gain).astype(jnp.bfloat16)
    values = value_raw.astype(jnp.bfloat16)
    head_size = key_gain.shape[-1]
    heads = queries.reshape(queries.shape[0], -1, head_size).astype(jnp.float32)
    scores = jnp.einsum("thd,jd->htj", heads, keys.astype(jnp.float32)) / math.sqrt(head_size)
    usable = jnp.arange(keys.shape[0]) < length
    scores = jnp.where(usable, scores, -1e30)
    scores = scores - jnp.max(scores, axis=-1, keepdims=True)
    expo = jnp.exp(scores)
    probs = (expo / jnp.sum(expo, axis=-1, keepdims=True)).astype(jnp.bfloat16)
    mixed = jnp.einsum("htj,jd->thd", probs.astype(jnp.float32), values.astype(jnp.float32))
    mixed = mixed.reshape(queries.shape[0], -1)
    shown = jnp.arange(queries.shape[0]) >= start
    return jnp.where(shown[:, None], mixed, 0.0)


def plain(layer_heads, queries, images, w_key, w_value, key_gain, d_out, img_len, text_start):
    image_full = lax.all_gather(images[0], "section", axis=0, tiled=True)
    layer = lax.axis_index("section") // layer_heads
    gain = lax.dynamic_index_in_dim(key_gain, layer, 0, keepdims=False)
    key_weight = lax.all_gather(w_key[0], "dp", axis=0, tiled=True)
    value_weight = lax.all_gather(w_value[0], "dp", axis=0, tiled=True)
    key_raw = jnp.dot(image_full, key_weight, preferred_element_type=jnp.float32)
    value_raw = jnp.dot(image_full, value_weight, preferred_element_type=jnp.float32)
    mixed, pull_back = jax.vjp(
        lambda kr, vr: attend(kr, vr, gain, queries[0], img_len[0], text_start[0]), key_raw, value_raw
    )
    d_key, d_value = pull_back(d_out[0].astype(jnp.float32))
    term = jnp.dot(d_key.astype(BF), key_weight.T, preferred_element_type=jnp.float32)
    term = term + jnp.dot(d_value.astype(BF), value_weight.T, preferred_element_type=jnp.float32)
    own = lax.psum_scatter(term.astype(BF), "section", scatter_dimension=0, tiled=True)
    return mixed.astype(BF)[None], own.astype(jnp.float32)[None]


def nt(a, b):
    return lax.dot_general(a, b, (((1,), (1,)), ((), ())), preferred_element_type=F32)


def kernel(
    n, m, layer_heads,
    len_hbm, start_hbm, gain_hbm, q_hbm, img_hbm, wk_hbm, wv_hbm, do_hbm,
    att_ref, grad_ref,
    len_ref, start_ref, gain_ref,
    img, wk, wv, q, do, exact, probs, term, stage, recv, kraw, vraw, dk, dv,
    local_sem, ag_send, ag_recv, w_send, w_recv, rs_send, rs_recv,
):
    half = n // 2
    s = lax.axis_index("section")
    g = lax.axis_index("dp")
    x = lax.rem(s, 2)
    pos = (1 - x) * lax.div(s, 2) + x * (n - 1 - lax.div(s, 2))

    def sec(offset):
        at = lax.rem(pos + offset + n, n)
        hi = lax.div(at, half)
        return (1 - hi) * 2 * at + hi * (2 * (n - 1 - at) + 1)

    def dp_flip(bit):
        return g + bit - 2 * bit * lax.rem(lax.div(g, bit), 2)

    def dp_xor(mask):
        at = g
        for k in range(m.bit_length() - 1):
            if mask & (1 << k):
                at = at + (1 << k) - 2 * (1 << k) * lax.rem(lax.div(g, 1 << k), 2)
        return at

    bits = [1 << k for k in reversed(range(m.bit_length() - 1))]
    right, left = sec(1), sec(-1)
    barrier = pltpu.get_barrier_semaphore()
    for neighbour in (left, right):
        pl.semaphore_signal(barrier, inc=1, device_id={"section": neighbour}, device_id_type=MESH)
    for bit in bits:
        pl.semaphore_signal(barrier, inc=1, device_id={"dp": dp_flip(bit)}, device_id_type=MESH)

    locals_ = [
        pltpu.make_async_copy(img_hbm.at[0], img.at[s], local_sem.at[0]),
        pltpu.make_async_copy(wk_hbm.at[0], wk.at[g], local_sem.at[1]),
        pltpu.make_async_copy(wv_hbm.at[0], wv.at[g], local_sem.at[2]),
        pltpu.make_async_copy(q_hbm.at[0], q, local_sem.at[3]),
        pltpu.make_async_copy(do_hbm.at[0], do, local_sem.at[4]),
        pltpu.make_async_copy(gain_hbm, gain_ref, local_sem.at[5]),
        pltpu.make_async_copy(len_hbm, len_ref, local_sem.at[6]),
        pltpu.make_async_copy(start_hbm, start_ref, local_sem.at[7]),
    ]
    pl.semaphore_wait(barrier, 2 + len(bits))

    cols = img.shape[2]
    part = cols // PARTS
    to = (right, left)

    def ag_copy(way, step, c):
        block = sec(-step if way == 0 else step)
        here = pl.ds(c * part, part)
        source = img_hbm.at[0, :, here] if step == 0 else img.at[block, :, here]
        return pltpu.make_async_remote_copy(
            src_ref=source,
            dst_ref=img.at[block, :, here],
            send_sem=ag_send.at[way, step, c],
            recv_sem=ag_recv.at[way, step, c],
            device_id={"section": to[way]},
            device_id_type=MESH,
        )

    def ag_arrival(way, step, c):
        block = sec(-step - 1 if way == 0 else step + 1)
        here = pl.ds(c * part, part)
        return pltpu.make_async_remote_copy(
            src_ref=img.at[block, :, here],
            dst_ref=img.at[block, :, here],
            send_sem=ag_send.at[way, step, c],
            recv_sem=ag_recv.at[way, step, c],
            device_id={"section": to[way]},
            device_id_type=MESH,
        )

    def ag_parts(way, step):
        if step < half - 1:
            return range(PARTS)
        cut = PARTS // 2
        return range(cut) if way == 0 else range(cut, PARTS)

    depth = wk.shape[1]
    cut = depth // W_PARTS
    w_list = []
    held = [0]
    for bit in bits:
        for mask in list(held):
            for which in range(2):
                for c in range(W_PARTS):
                    w_list.append((bit, mask, which, c))
            held.append(mask | bit)
    w_index = {item: k for k, item in enumerate(w_list)}

    def w_copy(bit, mask, which, c):
        k = w_index[(bit, mask, which, c)]
        block = dp_xor(mask)
        here = pl.ds(c * cut, cut)
        full, mine = ((wk, wk_hbm), (wv, wv_hbm))[which]
        return pltpu.make_async_remote_copy(
            src_ref=mine.at[0, here] if mask == 0 else full.at[block, here],
            dst_ref=full.at[block, here],
            send_sem=w_send.at[k],
            recv_sem=w_recv.at[k],
            device_id={"dp": dp_flip(bit)},
            device_id_type=MESH,
        )

    def w_take(bit, mask, which, c):
        k = w_index[(bit, mask, which, c)]
        here = pl.ds(c * cut, cut)
        landed = (wk, wv)[which].at[dp_xor(mask | bit), here]
        pltpu.make_async_remote_copy(
            src_ref=landed,
            dst_ref=landed,
            send_sem=w_send.at[k],
            recv_sem=w_recv.at[k],
            device_id={"dp": dp_flip(bit)},
            device_id_type=MESH,
        ).wait_recv()
        for low in bits:
            if low < bit:
                w_copy(low, mask | bit, which, c).start()

    far, near = bits
    tokens = n * img.shape[1]

    def project(mask, which=None):
        block = dp_xor(mask)
        columns = pl.ds(pl.multiple_of(block * depth, depth), depth)
        rows = img[:, :, columns].reshape(tokens, depth)
        if which is None:
            weight = jnp.concatenate([wk[block], wv[block]], axis=1)
            return jnp.dot(rows, weight, preferred_element_type=F32)
        return jnp.dot(rows, (wk, wv)[which][block], preferred_element_type=F32)

    for c in range(PARTS):
        for way in range(2):
            if c in ag_parts(way, 0):
                ag_copy(way, 0, c).start()
    for c in range(W_PARTS):
        w_copy(far, 0, 0, c).start()
    for which in range(2):
        for c in range(W_PARTS):
            w_copy(near, 0, which, c).start()
    for copy in locals_:
        copy.start()
    for step in range(1, half):
        for c in range(PARTS):
            for way in range(2):
                if c in ag_parts(way, step - 1):
                    ag_arrival(way, step - 1, c).wait_recv()
                    if c in ag_parts(way, step):
                        ag_copy(way, step, c).start()
        if step <= W_PARTS:
            w_copy(far, 0, 1, step - 1).start()
    for copy in locals_:
        copy.wait()
    for c in range(W_PARTS):
        w_take(far, 0, 0, c)
    for which in range(2):
        for c in range(W_PARTS):
            w_take(near, 0, which, c)
    for c in range(W_PARTS):
        w_take(near, far, 0, c)
    for c in range(W_PARTS - 1):
        w_take(far, 0, 1, c)
    for way in range(2):
        for c in ag_parts(way, half - 1):
            ag_arrival(way, half - 1, c).wait_recv()
    both = project(0) + project(near)
    w_take(far, 0, 1, W_PARTS - 1)
    both = both + project(far)

    size = kraw.shape[1]
    kraw[...] = both[:, :size] + project(far | near, 0)
    vraw[...] = both[:, size:]
    text = q.shape[0]
    heads = q.shape[1] // size
    layer = lax.div(s, layer_heads)
    gain = gain_ref[pl.ds(layer, 1), :]
    key_raw = kraw[...]
    inverse = lax.rsqrt(jnp.mean(key_raw * key_raw, axis=-1, keepdims=True) + 1e-05)
    keys = (key_raw * inverse * gain).astype(BF)
    usable = lax.broadcasted_iota(jnp.int32, (tokens, text), 0) < len_ref[0]
    shown = lax.broadcasted_iota(jnp.int32, (1, text), 1) >= start_ref[0]
    scale = 1.0 / math.sqrt(size)
    scale2 = scale * math.log2(math.e)

    def forward(h):
        at = pl.ds(h * size, size)
        scores = jnp.where(usable, nt(keys, q[:, at]) * scale2, -1e30)
        expo = jnp.exp2(scores - jnp.max(scores, axis=0, keepdims=True))
        factor = jnp.where(shown, 1.0 / jnp.sum(expo, axis=0, keepdims=True), 0.0)
        p = expo * factor
        half_p = p.astype(BF)
        exact[h] = p
        probs[h] = half_p
        return jnp.dot(half_p, do[:, at], preferred_element_type=F32)

    def backward(h):
        at = pl.ds(h * size, size)
        p = exact[h]
        d_p = nt(values, do[:, at]).astype(BF).astype(F32)
        d_s = (p * (d_p - jnp.sum(p * d_p, axis=0, keepdims=True))).astype(BF)
        return jnp.dot(d_s, q[:, at], preferred_element_type=F32)

    first_heads = heads // 2
    dv[...] = sum(forward(h) for h in range(first_heads))
    dv[...] += sum(forward(h) for h in range(first_heads, heads))
    for c in range(W_PARTS):
        w_take(near, far, 1, c)
    values = (vraw[...] + project(far | near, 1)).astype(BF)
    dk[...] = sum(backward(h) for h in range(first_heads))
    dk[...] += sum(backward(h) for h in range(first_heads, heads))
    d_keys = (dk[...] * scale).astype(BF).astype(F32) * gain
    d_key = inverse * (d_keys - key_raw * (inverse * inverse) * jnp.mean(d_keys * key_raw, axis=-1, keepdims=True))
    d_both = jnp.concatenate([d_key.astype(BF), dv[...].astype(BF)], axis=1)

    rows = img.shape[1]
    first = (list(range(m // 2)), list(range(m // 2, m)))
    later = (first[1] + first[0], first[0] + first[1])

    def rs_copy(way, step, c, source):
        here = pl.ds(c * depth, depth)
        return pltpu.make_async_remote_copy(
            src_ref=source.at[:, here],
            dst_ref=recv.at[way, step, :, here],
            send_sem=rs_send.at[way, step, c],
            recv_sem=rs_recv.at[way, step, c],
            device_id={"section": to[way]},
            device_id_type=MESH,
        )

    def target(way, step):
        return sec(half - step if way == 0 else step - half)

    order = [c for both in zip(*first) for c in both]
    for c in order:
        here = pl.ds(c * depth, depth)
        value = nt(d_both, jnp.concatenate([wk[c], wv[c]], axis=1))
        term[:, :, here] = value.astype(BF).reshape(n, rows, depth)
        for way in range(2):
            step = 0 if c in first[way] else 1
            if step < half:
                rs_copy(way, step, c, term.at[target(way, step)]).start()

    def mix(h):
        at = pl.ds(h * size, size)
        att_ref[0, :, at] = lax.dot_general(
            probs[h], values, (((0,), (0,)), ((), ())), preferred_element_type=F32
        ).astype(BF)

    to_mix = list(range(heads))
    for step in range(1, half):
        for k in range(m):
            if to_mix:
                mix(to_mix.pop(0))
            for way in range(2):
                c = later[way][k]
                if step == 1 and c not in first[way]:
                    continue
                here = pl.ds(c * depth, depth)
                rs_copy(way, step - 1, c, stage.at[way, step]).wait_recv()
                total = term[target(way, step), :, here].astype(F32) + recv[way, step - 1, :, here].astype(F32)
                stage[way, step, :, here] = total.astype(BF)
                rs_copy(way, step, c, stage.at[way, step]).start()
    while to_mix:
        mix(to_mix.pop(0))
    last = half - 1
    seen = []
    for k in range(m):
        for way in range(2):
            c = later[way][k]
            here = pl.ds(c * depth, depth)
            rs_copy(way, last, c, stage.at[way, last]).wait_recv()
            value = recv[way, last, :, here].astype(F32)
            if c not in seen:
                seen.append(c)
                grad_ref[0, :, here] = term[s, :, here].astype(F32) + value
            else:
                grad_ref[0, :, here] += value

    for step in range(half):
        for way in range(2):
            for c in ag_parts(way, step):
                ag_copy(way, step, c).wait_send()
    for item in w_list:
        w_copy(*item).wait_send()
    for step in range(half):
        for way in range(2):
            for c in first[way] if step == 0 else range(m):
                own = step == 0 or (step == 1 and c not in first[way])
                source = term.at[target(way, step)] if own else stage.at[way, step]
                rs_copy(way, step, c, source).wait_send()


def fused(n, m, layer_heads, queries, images, w_key, w_value, key_gain, d_out, img_len, text_start):
    _, text, width = queries.shape
    _, rows, d = images.shape
    _, depth, size = w_key.shape
    half = n // 2
    tokens = n * rows
    copies = 2 * (m - 1) * W_PARTS
    hbm = pl.BlockSpec(memory_space=pl.ANY)
    dma = pltpu.SemaphoreType.DMA
    return pl.pallas_call(
        functools.partial(kernel, n, m, layer_heads),
        out_shape=(
            pltpu.VMEM((1, text, width), BF),
            pltpu.VMEM((1, rows, d), F32),
        ),
        in_specs=[hbm] * 8,
        out_specs=(pl.BlockSpec(memory_space=pltpu.VMEM),) * 2,
        scratch_shapes=[
            pltpu.SMEM(img_len.shape, img_len.dtype),
            pltpu.SMEM(text_start.shape, text_start.dtype),
            pltpu.VMEM(key_gain.shape, key_gain.dtype),
            pltpu.VMEM((n, rows, d), BF),
            pltpu.VMEM((m, depth, size), BF),
            pltpu.VMEM((m, depth, size), BF),
            pltpu.VMEM((text, width), BF),
            pltpu.VMEM((text, width), BF),
            pltpu.VMEM((width // size, tokens, text), F32),
            pltpu.VMEM((width // size, tokens, text), BF),
            pltpu.VMEM((n, rows, d), BF),
            pltpu.VMEM((2, half, rows, d), BF),
            pltpu.VMEM((2, half, rows, d), BF),
            pltpu.VMEM((tokens, size), F32),
            pltpu.VMEM((tokens, size), F32),
            pltpu.VMEM((tokens, size), F32),
            pltpu.VMEM((tokens, size), F32),
            dma((8,)),
            dma((2, half, PARTS)),
            dma((2, half, PARTS)),
            dma((copies,)),
            dma((copies,)),
            dma((2, half, m)),
            dma((2, half, m)),
        ],
        compiler_params=pltpu.CompilerParams(
            collective_id=0, has_side_effects=True, vmem_limit_bytes=60 * 1024 * 1024
        ),
    )(img_len, text_start, key_gain, queries, images, w_key, w_value, d_out)


def solution(mesh):
    n, m = mesh.shape["section"], mesh.shape["dp"]

    def local(queries, images, w_key, w_value, key_gain, d_out, img_len, text_start):
        layer_heads = n * w_key.shape[0] // key_gain.shape[0]
        rows = images.shape[1]
        depth, size = w_key.shape[1:]
        heads = queries.shape[2] // size
        fits = (
            rows % 16 == 0 and depth % 128 == 0 and n >= 4 and n % 2 == 0
            and m == 4 and heads % 2 == 0
        )
        form = functools.partial(fused, n, m) if fits else plain
        return form(layer_heads, queries, images, w_key, w_value, key_gain, d_out, img_len, text_start)

    return jax.shard_map(
        local,
        mesh=mesh,
        in_specs=(
            P("section", "dp", None),
            P("dp", "section", None),
            P("section", "dp", None),
            P("section", "dp", None),
            P(),
            P("section", "dp", None),
            P("dp"),
            P("dp"),
        ),
        out_specs=(P("section", "dp", None), P("dp", "section", None)),
        check_vma=False,
    )
```
